32 devices in a mesh: tm: 16 (over z, y, x), space: 2 (over core).
Axes of the slice: x: 2, y: 2, z: 4, core: 2. Of those that a mesh axis runs over, the one named last changes fastest.
Arguments:
- snapshots: float32 [4096, 3, 1024], P('tm', None, 'space'), may hold values from -108 to 108
- weights: float32 [1024], P('space'), may hold values from 0.1 to 1
- start: float32 [2, 15, 8], replicated, may hold values from -6 to 6
Outputs:
- mode_out: float32 [64, 8, 2, 3, 1024], P('tm', None, None, None, 'space')
- energy: float32 [64, 8], P('tm')
The draws below stay inside these ranges and needn't reach their ends.
All inputs are finite; a program needn't handle non-finite values.
Results may differ from the reference program's by a relative error of at most 0.0003.
Values sent between devices are 32-bit elements; how exact they have to be, the bound alone decides.
A program may use at most 64 MiB of HBM per device.

```python
import math
import jax
import jax.numpy as jnp
from jax import lax

SEG = 256
NF = 64
K = 8
ITERS = 8
TIMES = 4096
BLOCKS = 15
POINTS = 1024


def draw_snapshots(key, part):
    key_noise, key_seg, key_point = jax.random.split(key, 3)
    seg_count = TIMES // SEG
    seg_scale = jnp.exp(jax.random.uniform(key_seg, (seg_count,), jnp.float32, math.log(0.5), math.log(2.0)))
    position = jnp.arange(POINTS, dtype=jnp.float32) / POINTS
    point_scale = jnp.exp(math.log(3.0) * position + jax.random.uniform(key_point, (POINTS,), jnp.float32, math.log(0.3), math.log(3.0)))
    noise = jnp.clip(jax.random.normal(key_noise, (TIMES, 3, POINTS), jnp.float32), -6.0, 6.0)
    return noise * jnp.repeat(seg_scale, SEG)[:, None, None] * point_scale[None, None, :]


def shard_levels(rng, dims, pieces, smallest, high):
    def one(dim, blocks):
        draws = jax.random.uniform(jax.random.fold_in(jax.random.fold_in(rng, 6), dim), (blocks,), jnp.float32, smallest / len(pieces), high / len(pieces))
        return jnp.repeat(jnp.exp(draws), dims[dim] // blocks).reshape((-1,) + (1,) * (len(dims) - dim - 1))

    loudness = one(*pieces[0])
    for cut in pieces[1:]:
        loudness = loudness * one(*cut)
    return loudness


def centred(rng, dims, spread, reach, held_as=jnp.bfloat16):
    result = spread * jax.random.normal(rng, dims, jnp.float32)
    return jnp.clip(result, min=-reach, max=reach).astype(held_as)


def setup_inputs(seed: int = 0) -> dict:
    arg_keys = jax.random.split(jax.random.key(seed), 4)
    snapshots = draw_snapshots(jax.random.fold_in(arg_keys[3], 71), 0)
    weights = jnp.clip(jnp.exp(math.log(1.0) - 2.3025851 * jax.random.uniform(arg_keys[1], (POINTS,), jnp.float32) ** shard_levels(arg_keys[1], (POINTS,), ((0, 2),), -0.2, 0.2)), 0.1, 1.0)
    start = centred(arg_keys[2], (2, BLOCKS, K), 1.0, 6.0, jnp.float32)
    return dict(snapshots=snapshots, weights=weights, start=start)


precise = lax.Precision.HIGHEST
epsilon = 1e-06

def dft_table(freqs, seg_len):
    length = 2 * seg_len
    times = jnp.arange(length, dtype=jnp.int32)
    freq_ids = jnp.arange(freqs, dtype=jnp.int32)
    turns = jnp.mod(freq_ids[:, None] * times[None, :], length).astype(jnp.float32)
    phase = 2.0 * math.pi / length * turns
    window = 0.5 - 0.5 * jnp.cos(2.0 * math.pi / length * times.astype(jnp.float32))
    factor = 1.0 / jnp.sqrt(jnp.sum(window * window))
    return jnp.concatenate([window * jnp.cos(phase) * factor, -window * jnp.sin(phase) * factor], 0)

def gram_parts(spectra, col_weights, total_points):
    weighted = spectra * col_weights
    grams = jnp.einsum('nrfc,msfc->frnsm', spectra, weighted, precision=precise)
    gram_re = (grams[:, 0, :, 0, :] + grams[:, 1, :, 1, :]) / total_points
    gram_im = (grams[:, 0, :, 1, :] - grams[:, 1, :, 0, :]) / total_points
    return (gram_re, gram_im)

def apply_gram(gram_re, gram_im, vec_re, vec_im):
    img_re = jnp.einsum('fnm,fmk->fnk', gram_re, vec_re, precision=precise) - jnp.einsum('fnm,fmk->fnk', gram_im, vec_im, precision=precise)
    img_im = jnp.einsum('fnm,fmk->fnk', gram_re, vec_im, precision=precise) + jnp.einsum('fnm,fmk->fnk', gram_im, vec_re, precision=precise)
    return (img_re, img_im)

def orthonormal(img_re, img_im):
    cols_re = []
    cols_im = []
    for column in range(img_re.shape[-1]):
        part_re = img_re[..., column]
        part_im = img_im[..., column]
        if column > 0:
            prev_re = jnp.stack(cols_re, -1)
            prev_im = jnp.stack(cols_im, -1)
            for repeat in range(2):
                coef_re = lax.optimization_barrier(jnp.sum(prev_re * part_re[..., None] + prev_im * part_im[..., None], axis=1))
                coef_im = lax.optimization_barrier(jnp.sum(prev_re * part_im[..., None] - prev_im * part_re[..., None], axis=1))
                part_re = part_re - lax.optimization_barrier(jnp.sum(prev_re * coef_re[:, None, :] - prev_im * coef_im[:, None, :], axis=-1))
                part_im = part_im - lax.optimization_barrier(jnp.sum(prev_re * coef_im[:, None, :] + prev_im * coef_re[:, None, :], axis=-1))
        inverse = 1.0 / jnp.sqrt(lax.optimization_barrier(jnp.sum(part_re * part_re + part_im * part_im, axis=1)) + epsilon)
        cols_re.append(part_re * inverse[:, None])
        cols_im.append(part_im * inverse[:, None])
    return (jnp.stack(cols_re, -1), jnp.stack(cols_im, -1))

def subspace(gram_re, gram_im, start):
    shape = (gram_re.shape[0], start.shape[1], start.shape[2])
    vec_re = jnp.broadcast_to(start[0], shape)
    vec_im = jnp.broadcast_to(start[1], shape)
    for sweep in range(ITERS):
        img_re, img_im = apply_gram(gram_re, gram_im, vec_re, vec_im)
        vec_re, vec_im = orthonormal(img_re, img_im)
    return (vec_re, vec_im)

def rayleigh(gram_re, gram_im, vec_re, vec_im):
    img_re, img_im = apply_gram(gram_re, gram_im, vec_re, vec_im)
    return lax.optimization_barrier(jnp.sum(vec_re * img_re + vec_im * img_im, axis=1))

def project(spectra, vec_re, vec_im):
    real_rows = spectra[:, 0]
    imag_rows = spectra[:, 1]
    mode_re = jnp.einsum('nfc,fnk->fkc', real_rows, vec_re, precision=precise) - jnp.einsum('nfc,fnk->fkc', imag_rows, vec_im, precision=precise)
    mode_im = jnp.einsum('nfc,fnk->fkc', real_rows, vec_im, precision=precise) + jnp.einsum('nfc,fnk->fkc', imag_rows, vec_re, precision=precise)
    return (mode_re, mode_im)

def reference(snapshots, weights, start):
    columns = 3 * POINTS
    samples = snapshots.reshape(TIMES, columns)
    basis = dft_table(NF, SEG)

    def one_block(index):
        rows = lax.dynamic_slice_in_dim(samples, index * SEG, 2 * SEG, 0)
        return jnp.dot(basis, rows, precision=precise)
    spectra = lax.map(one_block, jnp.arange(BLOCKS, dtype=jnp.int32))
    spectra = spectra.reshape(BLOCKS, 2, NF, columns)
    col_weights = jnp.tile(weights, 3)

    def one_freq(index):
        single = lax.dynamic_slice_in_dim(spectra, index, 1, 2)
        gram_re, gram_im = gram_parts(single, col_weights, POINTS)
        vec_re, vec_im = subspace(gram_re, gram_im, start)
        energy = rayleigh(gram_re, gram_im, vec_re, vec_im)
        mode_re, mode_im = project(single, vec_re, vec_im)
        inverse = 1.0 / jnp.sqrt(energy + epsilon)
        stacked = jnp.stack([mode_re, mode_im], 2) * inverse[:, :, None, None]
        return (stacked[0], energy[0])
    mode_out, energy = lax.map(one_freq, jnp.arange(NF, dtype=jnp.int32))
    return (mode_out.reshape(NF, K, 2, 3, POINTS), energy)
```

```python
import functools
import math

import numpy as np
import jax
import jax.numpy as jnp
from jax import lax
from jax.experimental import pallas as pl
from jax.experimental.pallas import tpu as pltpu
from jax.sharding import PartitionSpec as P

NF = 64
ITERS = 8

precise = lax.Precision.HIGHEST
epsilon = 1e-06


def segment_table(owners, seg_len):
    length = 2 * seg_len
    per = NF // owners
    t = np.arange(length)
    hann = 0.5 - 0.5 * np.cos(2.0 * np.pi / length * t)
    factor = 1.0 / np.sqrt(np.sum(hann * hann))
    freqs = np.arange(owners)[:, None] * per + np.arange(-1, per + 1)[None, :]
    turns = np.mod(freqs[:, :, None] * np.arange(seg_len), length)
    phase = 2.0 * np.pi / length * turns
    table = np.stack([np.cos(phase), -np.sin(phase)], 1) * factor
    return table.astype(np.float32)


def subspace_kernel(modes, mr_ref, mi_ref, start_ref, vec_ref, energy_ref):
    n = mr_ref.shape[0]

    def apply(vec):
        out = []
        for k in range(modes):
            vr, vi = vec[k]
            wr = wi = None
            for j in range(n):
                br, bi = vr[j : j + 1], vi[j : j + 1]
                ar, ai = mr_ref[j], mi_ref[j]
                pr, pi = ar * br - ai * bi, ar * bi + ai * br
                wr = pr if wr is None else wr + pr
                wi = pi if wi is None else wi + pi
            out.append((wr, wi))
        return out

    def total(x):
        return jnp.sum(x, axis=0, keepdims=True)

    def coefs(u, w):
        return total(u[0] * w[0] + u[1] * w[1]), total(u[0] * w[1] - u[1] * w[0])

    def less(w, u, c):
        return w[0] - (u[0] * c[0] - u[1] * c[1]), w[1] - (u[0] * c[1] + u[1] * c[0])

    def sweep(_, flat):
        vec = [(flat[2 * k], flat[2 * k + 1]) for k in range(modes)]
        images = apply(vec)
        rest = list(images)
        done = []
        for k in range(modes):
            w = rest[k]
            if done:
                cs = [coefs(u, w) for u in done]
                for u, c in zip(done, cs):
                    w = less(w, u, c)
            inverse = 1.0 / jnp.sqrt(total(w[0] * w[0] + w[1] * w[1]) + epsilon)
            u = (w[0] * inverse, w[1] * inverse)
            done.append(u)
            for later in range(k + 1, modes):
                rest[later] = less(rest[later], u, coefs(u, images[later]))
        return tuple(x for u in done for x in u)

    shape = mr_ref.shape[1:]
    flat = tuple(
        jnp.broadcast_to(start_ref[c, k], shape) for k in range(modes) for c in range(2)
    )
    flat = lax.fori_loop(0, ITERS, sweep, flat)
    vec = [(flat[2 * k], flat[2 * k + 1]) for k in range(modes)]
    images = apply(vec)
    for k in range(modes):
        (vr, vi), (wr, wi) = vec[k], images[k]
        energy = total(vr * wr + vi * wi)
        inverse = 1.0 / jnp.sqrt(energy + epsilon)
        energy_ref[k : k + 1] = energy
        vec_ref[0, k] = vr * inverse
        vec_ref[1, k] = vi * inverse


def subspace(gram_re, gram_im, start):
    freqs, n, _ = gram_re.shape
    modes = start.shape[2]
    start = jnp.pad(start, ((0, 0), (0, n - start.shape[1]), (0, 0)))
    start = start.transpose(0, 2, 1)[..., None]
    spec = pl.BlockSpec(memory_space=pltpu.VMEM)
    return pl.pallas_call(
        functools.partial(subspace_kernel, modes),
        out_shape=(
            jax.ShapeDtypeStruct((2, modes, n, freqs), jnp.float32),
            jax.ShapeDtypeStruct((modes, freqs), jnp.float32),
        ),
        in_specs=[spec] * 3,
        out_specs=(spec, spec),
    )(gram_re.transpose(2, 1, 0), gram_im.transpose(2, 1, 0), start)


def body(snapshots, weights, start):
    seg_len, components, points = snapshots.shape
    columns = components * points
    samples = snapshots.reshape(seg_len, columns)
    owners = lax.axis_size("tm")
    freqs = NF // owners
    table = segment_table(owners, seg_len)
    segment = jnp.dot(table.reshape(-1, seg_len), samples, precision=precise)
    arrived = lax.all_to_all(
        segment.reshape(owners, 2, freqs + 2, columns), "tm", split_axis=0, concat_axis=0, tiled=True
    )
    first = lax.axis_index("tm") * freqs - 1
    signs = 1.0 - 2.0 * jnp.mod(first + owners * freqs * 2 + jnp.arange(freqs + 2), 2).astype(jnp.float32)
    pairs = arrived[:-1] + signs[:, None] * arrived[1:]
    spectra = 0.5 * pairs[:, :, 1:-1] - 0.25 * (pairs[:, :, :-2] + pairs[:, :, 2:])
    blocks = owners - 1
    padded = (blocks + 7) // 8 * 8
    spectra = jnp.pad(spectra, ((0, padded - blocks), (0, 0), (0, 0), (0, 0)))
    col_weights = jnp.tile(weights, components)
    total_points = points * lax.axis_size("space")
    weighted = spectra * col_weights
    grams = jnp.einsum("nrfc,msfc->frnsm", spectra, weighted, precision=precise)
    gram_re = (grams[:, 0, :, 0, :] + grams[:, 1, :, 1, :]) / total_points
    gram_im = (grams[:, 0, :, 1, :] - grams[:, 1, :, 0, :]) / total_points
    gram_re, gram_im = lax.psum((gram_re, gram_im), "space")
    vec, energy = subspace(gram_re, gram_im, start)
    vr, vi = vec[0], vec[1]
    mix = jnp.stack([jnp.stack([vr, -vi], 0), jnp.stack([vi, vr], 0)], 0)
    modes = jnp.einsum("nrfc,srknf->fksc", spectra, mix, precision=precise)
    return modes.reshape(freqs, modes.shape[1], 2, components, points), energy.T


def solution(mesh):
    in_specs = (P("tm", None, "space"), P("space"), P())
    out_specs = (P("tm", None, None, None, "space"), P("tm", None))
    return jax.shard_map(body, mesh=mesh, in_specs=in_specs, out_specs=out_specs, check_vma=False)
```

```python
import functools
import math

import numpy as np
import jax
import jax.numpy as jnp
from jax import lax
from jax.experimental import pallas as pl
from jax.experimental.pallas import tpu as pltpu
from jax.sharding import PartitionSpec as P

NF = 64
ITERS = 8

precise = lax.Precision.HIGHEST
epsilon = 1e-06


def segment_table(owners, seg_len):
    length = 2 * seg_len
    per = NF // owners
    t = np.arange(length)
    hann = 0.5 - 0.5 * np.cos(2.0 * np.pi / length * t)
    factor = 1.0 / np.sqrt(np.sum(hann * hann))
    freqs = np.arange(owners)[:, None] * per + np.arange(-1, per + 1)[None, :]
    turns = np.mod(freqs[:, :, None] * np.arange(seg_len), length)
    phase = 2.0 * np.pi / length * turns
    table = np.stack([np.cos(phase), -np.sin(phase)], 1) * factor
    return table.astype(np.float32)


def exchange_kernel(table_ref, samples_ref, out_ref, send_ref, send_sems, recv_sems):
    owners, rows, half = send_ref.shape
    count = rows // 2
    points = samples_ref.shape[2]
    group = owners // 2
    me = lax.axis_index("tm")
    near = me // group
    far = 1 - near

    barrier = pltpu.get_barrier_semaphore()

    @pl.loop(1, owners)
    def _(s):
        other = lax.rem(me + s, owners)
        pl.semaphore_signal(barrier, inc=1, device_id={"tm": other}, device_id_type=pl.DeviceIdType.MESH)

    def transform(side):
        for c in range(samples_ref.shape[0]):
            part = jnp.dot(
                table_ref[side],
                samples_ref[c],
                precision=precise,
                preferred_element_type=jnp.float32,
            )
            low, high = c * points, (c + 1) * points
            for q in range(2):
                begin, end = max(low, q * half), min(high, (q + 1) * half)
                if begin >= end:
                    continue
                for i in range(group):
                    send_ref[
                        side * group + i, q * count : (q + 1) * count, begin - q * half : end - q * half
                    ] = part[i * count : (i + 1) * count, begin - low : end - low]

    def copy(source, target):
        return pltpu.make_async_remote_copy(
            src_ref=send_ref.at[target],
            dst_ref=out_ref.at[source],
            send_sem=send_sems.at[target],
            recv_sem=recv_sems.at[source],
            device_id={"tm": target},
            device_id_type=pl.DeviceIdType.MESH,
        )

    transform(far)
    pl.semaphore_wait(barrier, owners - 1)

    @pl.loop(0, group)
    def _(s):
        copy(me, far * group + lax.rem(me + s, group)).start()

    transform(near)

    @pl.loop(1, group)
    def _(s):
        copy(me, near * group + lax.rem(me + s, group)).start()

    out_ref[me] = send_ref[me]

    @pl.loop(1, owners)
    def _(s):
        other = lax.rem(me + s, owners)
        copy(me, other).wait_send()
        pltpu.make_async_remote_copy(
            src_ref=send_ref.at[other],
            dst_ref=out_ref.at[other],
            send_sem=send_sems.at[other],
            recv_sem=recv_sems.at[other],
            device_id={"tm": other},
            device_id_type=pl.DeviceIdType.MESH,
        ).wait_recv()


def exchange(table, samples):
    owners, parts, freqs, seg_len = table.shape
    half = samples.shape[0] * samples.shape[2] // 2
    rows = 2 * parts * freqs
    spec = pl.BlockSpec(memory_space=pltpu.VMEM)
    return pl.pallas_call(
        exchange_kernel,
        out_shape=jax.ShapeDtypeStruct((owners, rows, half), jnp.float32),
        in_specs=[spec] * 2,
        out_specs=spec,
        scratch_shapes=[
            pltpu.VMEM((owners, rows, half), jnp.float32),
            pltpu.SemaphoreType.DMA((owners,)),
            pltpu.SemaphoreType.DMA((owners,)),
        ],
        compiler_params=pltpu.CompilerParams(
            collective_id=0, has_side_effects=True, vmem_limit_bytes=40 * 1024 * 1024
        ),
    )(table.reshape(2, -1, seg_len), samples)


def subspace_kernel(modes, mr_ref, mi_ref, start_ref, vec_ref, energy_ref):
    n = mr_ref.shape[0]

    def apply(vec):
        out = []
        for k in range(modes):
            vr, vi = vec[k]
            wr = wi = None
            for j in range(n):
                br, bi = vr[j : j + 1], vi[j : j + 1]
                ar, ai = mr_ref[j], mi_ref[j]
                pr, pi = ar * br - ai * bi, ar * bi + ai * br
                wr = pr if wr is None else wr + pr
                wi = pi if wi is None else wi + pi
            out.append((wr, wi))
        return out

    def total(x):
        return jnp.sum(x, axis=0, keepdims=True)

    def coefs(u, w):
        return total(u[0] * w[0] + u[1] * w[1]), total(u[0] * w[1] - u[1] * w[0])

    def less(w, u, c):
        return w[0] - (u[0] * c[0] - u[1] * c[1]), w[1] - (u[0] * c[1] + u[1] * c[0])

    def sweep(_, flat):
        vec = [(flat[2 * k], flat[2 * k + 1]) for k in range(modes)]
        images = apply(vec)
        rest = list(images)
        done = []
        for k in range(modes):
            w = rest[k]
            if done:
                cs = [coefs(u, w) for u in done]
                for u, c in zip(done, cs):
                    w = less(w, u, c)
            inverse = 1.0 / jnp.sqrt(total(w[0] * w[0] + w[1] * w[1]) + epsilon)
            u = (w[0] * inverse, w[1] * inverse)
            done.append(u)
            for later in range(k + 1, modes):
                rest[later] = less(rest[later], u, coefs(u, images[later]))
        return tuple(x for u in done for x in u)

    shape = mr_ref.shape[1:]
    flat = tuple(
        jnp.broadcast_to(start_ref[c, k], shape) for k in range(modes) for c in range(2)
    )
    flat = lax.fori_loop(0, ITERS, sweep, flat)
    vec = [(flat[2 * k], flat[2 * k + 1]) for k in range(modes)]
    images = apply(vec)
    for k in range(modes):
        (vr, vi), (wr, wi) = vec[k], images[k]
        energy = total(vr * wr + vi * wi)
        inverse = 1.0 / jnp.sqrt(energy + epsilon)
        energy_ref[k : k + 1] = energy
        vec_ref[0, k] = vr * inverse
        vec_ref[1, k] = vi * inverse


def subspace(gram_re, gram_im, start):
    freqs, n, _ = gram_re.shape
    modes = start.shape[2]
    start = jnp.pad(start, ((0, 0), (0, n - start.shape[1]), (0, 0)))
    start = start.transpose(0, 2, 1)[..., None]
    spec = pl.BlockSpec(memory_space=pltpu.VMEM)
    return pl.pallas_call(
        functools.partial(subspace_kernel, modes),
        out_shape=(
            jax.ShapeDtypeStruct((2, modes, n, freqs), jnp.float32),
            jax.ShapeDtypeStruct((modes, freqs), jnp.float32),
        ),
        in_specs=[spec] * 3,
        out_specs=(spec, spec),
    )(gram_re.transpose(2, 1, 0), gram_im.transpose(2, 1, 0), start)


def body(snapshots, weights, start):
    seg_len, components, points = snapshots.shape
    columns = components * points
    samples = snapshots.transpose(1, 0, 2)
    owners = lax.axis_size("tm")
    freqs = NF // owners
    table = segment_table(owners, seg_len)
    arrived = exchange(table, samples).reshape(owners, 2, 2, freqs + 2, columns // 2)
    first = lax.axis_index("tm") * freqs - 1
    signs = 1.0 - 2.0 * jnp.mod(first + owners * freqs * 2 + jnp.arange(freqs + 2), 2).astype(jnp.float32)
    pairs = arrived[:-1] + signs[:, None] * arrived[1:]
    spectra = 0.5 * pairs[..., 1:-1, :] - 0.25 * (pairs[..., :-2, :] + pairs[..., 2:, :])
    spectra = jnp.concatenate([spectra[:, 0], spectra[:, 1]], -1)
    blocks = owners - 1
    padded = (blocks + 7) // 8 * 8
    spectra = jnp.pad(spectra, ((0, padded - blocks), (0, 0), (0, 0), (0, 0)))
    col_weights = jnp.tile(weights, components)
    total_points = points * lax.axis_size("space")
    weighted = spectra * col_weights
    grams = jnp.einsum("nrfc,msfc->frnsm", spectra, weighted, precision=precise)
    gram_re = (grams[:, 0, :, 0, :] + grams[:, 1, :, 1, :]) / total_points
    gram_im = (grams[:, 0, :, 1, :] - grams[:, 1, :, 0, :]) / total_points
    gram_re, gram_im = lax.psum((gram_re, gram_im), "space")
    vec, energy = subspace(gram_re, gram_im, start)
    vr, vi = vec[0], vec[1]
    mix = jnp.stack([jnp.stack([vr, -vi], 0), jnp.stack([vi, vr], 0)], 0)
    modes = jnp.einsum("nrfc,srknf->fksc", spectra, mix, precision=precise)
    return modes.reshape(freqs, modes.shape[1], 2, components, points), energy.T


def solution(mesh):
    in_specs = (P("tm", None, "space"), P("space"), P())
    out_specs = (P("tm", None, None, None, "space"), P("tm", None))
    return jax.shard_map(body, mesh=mesh, in_specs=in_specs, out_specs=out_specs, check_vma=False)
```

```python
import functools
import math

import numpy as np
import jax
import jax.numpy as jnp
from jax import lax
from jax.experimental import pallas as pl
from jax.experimental.pallas import tpu as pltpu
from jax.sharding import PartitionSpec as P

NF = 64
ITERS = 8

precise = lax.Precision.HIGHEST
epsilon = 1e-06


def segment_table(owners, seg_len):
    length = 2 * seg_len
    per = NF // owners
    t = np.arange(length)
    hann = 0.5 - 0.5 * np.cos(2.0 * np.pi / length * t)
    factor = 1.0 / np.sqrt(np.sum(hann * hann))
    freqs = np.arange(owners)[:, None] * per + np.arange(-1, per + 1)[None, :]
    turns = np.mod(freqs[:, :, None] * np.arange(seg_len), length)
    phase = 2.0 * np.pi / length * turns
    table = np.stack([np.cos(phase), -np.sin(phase)], 1) * factor
    return table.astype(np.float32)


def exchange_kernel(
    table_ref, samples_ref, main_ref, edges_ref, main_out, edge_out, forward_out,
    main_send, main_recv, edge_send, edge_recv, forward_send, forward_recv, last_send,
):
    owners, count, _ = main_ref.shape
    freqs = count // 2
    points = samples_ref.shape[2]
    quarter = edges_ref.shape[3]
    group = owners // 2
    me = lax.axis_index("tm")
    near = me // group
    far = 1 - near
    last = owners - 1

    barrier = pltpu.get_barrier_semaphore()

    @pl.loop(1, owners)
    def _(s):
        other = lax.rem(me + s, owners)
        pl.semaphore_signal(barrier, inc=1, device_id={"tm": other}, device_id_type=pl.DeviceIdType.MESH)

    def remote(source, target, sent, received, device):
        return pltpu.make_async_remote_copy(
            src_ref=source,
            dst_ref=target,
            send_sem=sent,
            recv_sem=received,
            device_id={"tm": device},
            device_id_type=pl.DeviceIdType.MESH,
        )

    def transform(side, edged):
        for c in range(samples_ref.shape[0]):
            part = jnp.dot(
                table_ref[side],
                samples_ref[c],
                precision=precise,
                preferred_element_type=jnp.float32,
            )
            low, high = c * points, (c + 1) * points
            for i in range(group):
                main_out[side * group + i, :, low:high] = part[i * count : (i + 1) * count]
            for q in range(4):
                begin, end = max(low, q * quarter), min(high, (q + 1) * quarter)
                if begin >= end:
                    continue
                for i in edged:
                    for edge in range(2):
                        for r in range(2):
                            row = group * count + i * 4 + edge * 2 + r
                            edge_out[
                                side * group + i,
                                edge,
                                r * 4 + q : r * 4 + q + 1,
                                begin - q * quarter : end - q * quarter,
                            ] = part[row : row + 1, begin - low : end - low]

    def main_copy(slot, device):
        return remote(main_out.at[device], main_ref.at[slot], main_send.at[device], main_recv.at[slot], device)

    def edge_copy(slot, device):
        return remote(edge_out.at[device], edges_ref.at[slot], edge_send.at[device], edge_recv.at[slot], device)

    def last_copy():
        return remote(
            edge_out.at[last, 1], edges_ref.at[me, 1], last_send.at[0], forward_recv.at[me, 1], last
        )

    def forward_copy(source, edge, device):
        return remote(
            forward_out.at[source, edge],
            edges_ref.at[source, edge],
            forward_send.at[source, edge],
            forward_recv.at[source, edge],
            device,
        )

    def pack(target, source, edge, freq, sign):
        for r in range(2):
            for q in range(4):
                row = main_ref[source, r * freqs + freq : r * freqs + freq + 1, q * quarter : (q + 1) * quarter]
                target[source, edge, r * 4 + q : r * 4 + q + 1, :] = row if r == 0 else sign * row

    transform(far, [group - 1])
    pl.semaphore_wait(barrier, owners - 1)

    @pl.loop(0, group)
    def _(s):
        main_copy(me, far * group + lax.rem(me + s, group)).start()

    @pl.when(near == 0)
    def _():
        last_copy().start()

    transform(near, range(group))

    @pl.loop(1, group)
    def _(s):
        other = near * group + lax.rem(me + s, group)
        main_copy(me, other).start()
        edge_copy(me, other).start()

    main_ref[me] = main_out[me]
    edges_ref[me] = edge_out[me]

    lower = me - 1
    upper = me + 1
    inner_lower = jnp.logical_and(me > 0, lower // group == near)
    inner_upper = jnp.logical_and(me < last, upper // group == near)
    outer_lower = jnp.logical_and(me > 0, lower // group != near)
    outer_upper = jnp.logical_and(me < last, upper // group != near)

    def forward(source, to_lower, to_upper):
        @pl.when(to_lower)
        def _():
            pack(forward_out, source, 1, 0, 1.0)
            forward_copy(source, 1, lower).start()

        @pl.when(to_upper)
        def _():
            pack(forward_out, source, 0, freqs - 1, 1.0)
            forward_copy(source, 0, upper).start()

    @pl.loop(0, group)
    def _(s):
        source = far * group + lax.rem(me - s + owners, group)
        main_copy(source, source).wait_recv()
        forward(source, inner_lower, inner_upper)

    forward(me, outer_lower, outer_upper)

    @pl.loop(1, group)
    def _(s):
        source = near * group + lax.rem(me - s + owners, group)
        main_copy(source, source).wait_recv()
        edge_copy(source, source).wait_recv()
        forward(source, outer_lower, outer_upper)

    @pl.loop(0, group)
    def _(s):
        source = far * group + s
        main_copy(me, source).wait_send()
        forward_copy(source, 1, lower).wait_recv()

        @pl.when(me > 0)
        def _():
            forward_copy(source, 0, upper).wait_recv()

        @pl.when(me == 0)
        def _():
            if freqs > 1:
                pack(edges_ref, source, 0, 1, -1.0)
            else:
                edges_ref[source, 0, 0:4] = edges_ref[source, 1, 0:4]
                edges_ref[source, 0, 4:8] = -edges_ref[source, 1, 4:8]

        @pl.when(inner_lower)
        def _():
            forward_copy(source, 1, lower).wait_send()

        @pl.when(inner_upper)
        def _():
            forward_copy(source, 0, upper).wait_send()

    @pl.loop(0, group)
    def _(s):
        source = near * group + s

        @pl.when(source != me)
        def _():
            main_copy(me, source).wait_send()
            edge_copy(me, source).wait_send()

        @pl.when(outer_lower)
        def _():
            forward_copy(source, 1, lower).wait_send()

        @pl.when(outer_upper)
        def _():
            forward_copy(source, 0, upper).wait_send()

    @pl.when(near == 0)
    def _():
        last_copy().wait_send()


def exchange(table, samples):
    owners, parts, freqs, seg_len = table.shape
    group = owners // 2
    columns = samples.shape[0] * samples.shape[2]
    main = table[:, :, 1:-1].reshape(2, -1, seg_len)
    edge = table[:, :, [0, freqs - 1]].swapaxes(1, 2).reshape(2, -1, seg_len)
    rows = np.concatenate([main, edge], 1)
    main_shape = (owners, parts * (freqs - 2), columns)
    edge_shape = (owners, 2, 8, columns // 4)
    spec = pl.BlockSpec(memory_space=pltpu.VMEM)
    return pl.pallas_call(
        exchange_kernel,
        out_shape=(
            jax.ShapeDtypeStruct(main_shape, jnp.float32),
            jax.ShapeDtypeStruct(edge_shape, jnp.float32),
        ),
        in_specs=[spec] * 2,
        out_specs=(spec, spec),
        scratch_shapes=[
            pltpu.VMEM(main_shape, jnp.float32),
            pltpu.VMEM(edge_shape, jnp.float32),
            pltpu.VMEM(edge_shape, jnp.float32),
            pltpu.SemaphoreType.DMA((owners,)),
            pltpu.SemaphoreType.DMA((owners,)),
            pltpu.SemaphoreType.DMA((owners,)),
            pltpu.SemaphoreType.DMA((owners,)),
            pltpu.SemaphoreType.DMA((owners, 2)),
            pltpu.SemaphoreType.DMA((owners, 2)),
            pltpu.SemaphoreType.DMA((1,)),
        ],
        compiler_params=pltpu.CompilerParams(
            collective_id=0, has_side_effects=True, vmem_limit_bytes=40 * 1024 * 1024
        ),
    )(rows, samples)


def subspace_kernel(modes, mr_ref, mi_ref, start_ref, vec_ref, energy_ref):
    n = mr_ref.shape[0]

    def apply(vec):
        out = []
        for k in range(modes):
            vr, vi = vec[k]
            wr = wi = None
            for j in range(n):
                br, bi = vr[j : j + 1], vi[j : j + 1]
                ar, ai = mr_ref[j], mi_ref[j]
                pr, pi = ar * br - ai * bi, ar * bi + ai * br
                wr = pr if wr is None else wr + pr
                wi = pi if wi is None else wi + pi
            out.append((wr, wi))
        return out

    def total(x):
        return jnp.sum(x, axis=0, keepdims=True)

    def coefs(u, w):
        return total(u[0] * w[0] + u[1] * w[1]), total(u[0] * w[1] - u[1] * w[0])

    def less(w, u, c):
        return w[0] - (u[0] * c[0] - u[1] * c[1]), w[1] - (u[0] * c[1] + u[1] * c[0])

    def sweep(_, flat):
        vec = [(flat[2 * k], flat[2 * k + 1]) for k in range(modes)]
        images = apply(vec)
        rest = list(images)
        done = []
        for k in range(modes):
            w = rest[k]
            if done:
                cs = [coefs(u, w) for u in done]
                for u, c in zip(done, cs):
                    w = less(w, u, c)
            inverse = 1.0 / jnp.sqrt(total(w[0] * w[0] + w[1] * w[1]) + epsilon)
            u = (w[0] * inverse, w[1] * inverse)
            done.append(u)
            for later in range(k + 1, modes):
                rest[later] = less(rest[later], u, coefs(u, images[later]))
        return tuple(x for u in done for x in u)

    shape = mr_ref.shape[1:]
    flat = tuple(
        jnp.broadcast_to(start_ref[c, k], shape) for k in range(modes) for c in range(2)
    )
    flat = lax.fori_loop(0, ITERS, sweep, flat)
    vec = [(flat[2 * k], flat[2 * k + 1]) for k in range(modes)]
    images = apply(vec)
    for k in range(modes):
        (vr, vi), (wr, wi) = vec[k], images[k]
        energy = total(vr * wr + vi * wi)
        inverse = 1.0 / jnp.sqrt(energy + epsilon)
        energy_ref[k : k + 1] = energy
        vec_ref[0, k] = vr * inverse
        vec_ref[1, k] = vi * inverse


def subspace(gram_re, gram_im, start):
    freqs, n, _ = gram_re.shape
    modes = start.shape[2]
    start = jnp.pad(start, ((0, 0), (0, n - start.shape[1]), (0, 0)))
    start = start.transpose(0, 2, 1)[..., None]
    spec = pl.BlockSpec(memory_space=pltpu.VMEM)
    return pl.pallas_call(
        functools.partial(subspace_kernel, modes),
        out_shape=(
            jax.ShapeDtypeStruct((2, modes, n, freqs), jnp.float32),
            jax.ShapeDtypeStruct((modes, freqs), jnp.float32),
        ),
        in_specs=[spec] * 3,
        out_specs=(spec, spec),
    )(gram_re.transpose(2, 1, 0), gram_im.transpose(2, 1, 0), start)


def body(snapshots, weights, start):
    seg_len, components, points = snapshots.shape
    columns = components * points
    samples = snapshots.transpose(1, 0, 2)
    owners = lax.axis_size("tm")
    freqs = NF // owners
    table = segment_table(owners, seg_len)
    main, edges = exchange(table, samples)
    main = main.reshape(owners, 2, freqs, columns)
    edges = edges.reshape(owners, 2, 2, 1, columns)
    arrived = jnp.concatenate([edges[:, 0], main, edges[:, 1]], 2)
    first = lax.axis_index("tm") * freqs - 1
    signs = 1.0 - 2.0 * jnp.mod(first + owners * freqs * 2 + jnp.arange(freqs + 2), 2).astype(jnp.float32)
    pairs = arrived[:-1] + signs[:, None] * arrived[1:]
    spectra = 0.5 * pairs[..., 1:-1, :] - 0.25 * (pairs[..., :-2, :] + pairs[..., 2:, :])
    blocks = owners - 1
    padded = (blocks + 7) // 8 * 8
    spectra = jnp.pad(spectra, ((0, padded - blocks), (0, 0), (0, 0), (0, 0)))
    col_weights = jnp.tile(weights, components)
    total_points = points * lax.axis_size("space")
    weighted = spectra * col_weights
    grams = jnp.einsum("nrfc,msfc->frnsm", spectra, weighted, precision=precise)
    gram_re = (grams[:, 0, :, 0, :] + grams[:, 1, :, 1, :]) / total_points
    gram_im = (grams[:, 0, :, 1, :] - grams[:, 1, :, 0, :]) / total_points
    gram_re, gram_im = lax.psum((gram_re, gram_im), "space")
    vec, energy = subspace(gram_re, gram_im, start)
    vr, vi = vec[0], vec[1]
    mix = jnp.stack([jnp.stack([vr, -vi], 0), jnp.stack([vi, vr], 0)], 0)
    modes = jnp.einsum("nrfc,srknf->fksc", spectra, mix, precision=precise)
    return modes.reshape(freqs, modes.shape[1], 2, components, points), energy.T


def solution(mesh):
    in_specs = (P("tm", None, "space"), P("space"), P())
    out_specs = (P("tm", None, None, None, "space"), P("tm", None))
    return jax.shard_map(body, mesh=mesh, in_specs=in_specs, out_specs=out_specs, check_vma=False)
```

```python
import functools
import math

import numpy as np
import jax
import jax.numpy as jnp
from jax import lax
from jax.experimental import pallas as pl
from jax.experimental.pallas import tpu as pltpu
from jax.sharding import PartitionSpec as P

NF = 64
ITERS = 8

precise = lax.Precision.HIGHEST
epsilon = 1e-06


def segment_table(owners, seg_len):
    length = 2 * seg_len
    per = NF // owners
    t = np.arange(length)
    hann = 0.5 - 0.5 * np.cos(2.0 * np.pi / length * t)
    factor = 1.0 / np.sqrt(np.sum(hann * hann))
    freqs = np.arange(owners)[:, None] * per + np.arange(-1, per + 1)[None, :]
    turns = np.mod(freqs[:, :, None] * np.arange(seg_len), length)
    phase = 2.0 * np.pi / length * turns
    table = np.stack([np.cos(phase), -np.sin(phase)], 1) * factor
    return table.astype(np.float32)


def exchange_kernel(
    table_ref, samples_ref, main_ref, edges_ref, main_out, edge_out, forward_out,
    main_send, main_recv, edge_send, edge_recv, forward_send, forward_recv, last_send,
):
    owners, count, _ = main_ref.shape
    freqs = count // 2
    points = samples_ref.shape[2]
    quarter = edges_ref.shape[3]
    group = owners // 2
    me = lax.axis_index("tm")
    near = me // group
    far = 1 - near
    last = owners - 1

    barrier = pltpu.get_barrier_semaphore()

    @pl.loop(1, owners)
    def _(s):
        other = lax.rem(me + s, owners)
        pl.semaphore_signal(barrier, inc=1, device_id={"tm": other}, device_id_type=pl.DeviceIdType.MESH)

    def remote(source, target, sent, received, device):
        return pltpu.make_async_remote_copy(
            src_ref=source,
            dst_ref=target,
            send_sem=sent,
            recv_sem=received,
            device_id={"tm": device},
            device_id_type=pl.DeviceIdType.MESH,
        )

    def transform(side, edged):
        for c in range(samples_ref.shape[0]):
            part = jnp.dot(
                table_ref[side],
                samples_ref[c],
                precision=precise,
                preferred_element_type=jnp.float32,
            )
            low, high = c * points, (c + 1) * points
            for i in range(group):
                main_out[side * group + i, :, low:high] = part[i * count : (i + 1) * count]
            for q in range(4):
                begin, end = max(low, q * quarter), min(high, (q + 1) * quarter)
                if begin >= end:
                    continue
                for i in edged:
                    for edge in range(2):
                        for r in range(2):
                            row = group * count + i * 4 + edge * 2 + r
                            edge_out[
                                side * group + i,
                                edge,
                                r * 4 + q : r * 4 + q + 1,
                                begin - q * quarter : end - q * quarter,
                            ] = part[row : row + 1, begin - low : end - low]

    def main_copy(slot, device):
        return remote(main_out.at[device], main_ref.at[slot], main_send.at[device], main_recv.at[slot], device)

    def edge_copy(slot, device):
        return remote(edge_out.at[device], edges_ref.at[slot], edge_send.at[device], edge_recv.at[slot], device)

    def last_copy():
        return remote(
            edge_out.at[last, 1], edges_ref.at[me, 1], last_send.at[0], forward_recv.at[me, 1], last
        )

    def forward_copy(source, edge, device):
        return remote(
            forward_out.at[source, edge],
            edges_ref.at[source, edge],
            forward_send.at[source, edge],
            forward_recv.at[source, edge],
            device,
        )

    def pack(target, source, edge, freq, sign):
        for r in range(2):
            for q in range(4):
                row = main_ref[source, r * freqs + freq : r * freqs + freq + 1, q * quarter : (q + 1) * quarter]
                target[source, edge, r * 4 + q : r * 4 + q + 1, :] = row if r == 0 else sign * row

    transform(far, [group - 1])
    pl.semaphore_wait(barrier, owners - 1)

    @pl.loop(0, group)
    def _(s):
        main_copy(me, far * group + lax.rem(me + s, group)).start()

    @pl.when(near == 0)
    def _():
        last_copy().start()

    transform(near, range(group))

    @pl.loop(1, group)
    def _(s):
        other = near * group + lax.rem(me + s, group)
        main_copy(me, other).start()
        edge_copy(me, other).start()

    main_ref[me] = main_out[me]
    edges_ref[me] = edge_out[me]

    lower = me - 1
    upper = me + 1
    inner_lower = jnp.logical_and(me > 0, lower // group == near)
    inner_upper = jnp.logical_and(me < last, upper // group == near)
    outer_lower = jnp.logical_and(me > 0, lower // group != near)
    outer_upper = jnp.logical_and(me < last, upper // group != near)

    def forward(source, to_lower, to_upper):
        @pl.when(to_lower)
        def _():
            pack(forward_out, source, 1, 0, 1.0)
            forward_copy(source, 1, lower).start()

        @pl.when(to_upper)
        def _():
            pack(forward_out, source, 0, freqs - 1, 1.0)
            forward_copy(source, 0, upper).start()

    @pl.loop(0, group)
    def _(s):
        source = far * group + lax.rem(me - s + owners, group)
        main_copy(source, source).wait_recv()
        forward(source, inner_lower, inner_upper)

    forward(me, outer_lower, outer_upper)

    @pl.loop(1, group)
    def _(s):
        source = near * group + lax.rem(me - s + owners, group)
        main_copy(source, source).wait_recv()
        edge_copy(source, source).wait_recv()
        forward(source, outer_lower, outer_upper)

    @pl.loop(0, group)
    def _(s):
        source = far * group + s
        main_copy(me, source).wait_send()
        forward_copy(source, 1, lower).wait_recv()

        @pl.when(me > 0)
        def _():
            forward_copy(source, 0, upper).wait_recv()

        @pl.when(me == 0)
        def _():
            if freqs > 1:
                pack(edges_ref, source, 0, 1, -1.0)
            else:
                edges_ref[source, 0, 0:4] = edges_ref[source, 1, 0:4]
                edges_ref[source, 0, 4:8] = -edges_ref[source, 1, 4:8]

        @pl.when(inner_lower)
        def _():
            forward_copy(source, 1, lower).wait_send()

        @pl.when(inner_upper)
        def _():
            forward_copy(source, 0, upper).wait_send()

    @pl.loop(0, group)
    def _(s):
        source = near * group + s

        @pl.when(source != me)
        def _():
            main_copy(me, source).wait_send()
            edge_copy(me, source).wait_send()

        @pl.when(outer_lower)
        def _():
            forward_copy(source, 1, lower).wait_send()

        @pl.when(outer_upper)
        def _():
            forward_copy(source, 0, upper).wait_send()

    @pl.when(near == 0)
    def _():
        last_copy().wait_send()


def exchange(table, samples):
    owners, parts, freqs, seg_len = table.shape
    group = owners // 2
    columns = samples.shape[0] * samples.shape[2]
    main = table[:, :, 1:-1].reshape(2, -1, seg_len)
    edge = table[:, :, [0, freqs - 1]].swapaxes(1, 2).reshape(2, -1, seg_len)
    rows = np.concatenate([main, edge], 1)
    main_shape = (owners, parts * (freqs - 2), columns)
    edge_shape = (owners, 2, 8, columns // 4)
    spec = pl.BlockSpec(memory_space=pltpu.VMEM)
    return pl.pallas_call(
        exchange_kernel,
        out_shape=(
            jax.ShapeDtypeStruct(main_shape, jnp.float32),
            jax.ShapeDtypeStruct(edge_shape, jnp.float32),
        ),
        in_specs=[spec] * 2,
        out_specs=(spec, spec),
        scratch_shapes=[
            pltpu.VMEM(main_shape, jnp.float32),
            pltpu.VMEM(edge_shape, jnp.float32),
            pltpu.VMEM(edge_shape, jnp.float32),
            pltpu.SemaphoreType.DMA((owners,)),
            pltpu.SemaphoreType.DMA((owners,)),
            pltpu.SemaphoreType.DMA((owners,)),
            pltpu.SemaphoreType.DMA((owners,)),
            pltpu.SemaphoreType.DMA((owners, 2)),
            pltpu.SemaphoreType.DMA((owners, 2)),
            pltpu.SemaphoreType.DMA((1,)),
        ],
        compiler_params=pltpu.CompilerParams(
            collective_id=0, has_side_effects=True, vmem_limit_bytes=40 * 1024 * 1024
        ),
    )(rows, samples)


def modes_kernel(
    modes, total_points, spectra_ref, weights_ref, start_ref, out_ref, energy_ref,
    gram_ref, mine_ref, mr_ref, mi_ref, send_sems, recv_sems,
):
    freqs, double, columns = spectra_ref.shape
    n = double // 2
    lanes = freqs * double
    devices = gram_ref.shape[0]
    me = lax.axis_index("space")

    barrier = pltpu.get_barrier_semaphore()
    for s in range(1, devices):
        other = lax.rem(me + s, devices)
        pl.semaphore_signal(barrier, inc=1, device_id={"space": other}, device_id_type=pl.DeviceIdType.MESH)

    rows = spectra_ref[...].reshape(lanes, columns)
    grams = lax.dot_general(
        rows,
        rows * weights_ref[...],
        (((1,), (1,)), ((), ())),
        precision=precise,
        preferred_element_type=jnp.float32,
    )
    owner = lax.broadcasted_iota(jnp.int32, (n, lanes), 1) // double
    top = grams[:n]
    low = grams[n:double]
    for f in range(1, freqs):
        top = jnp.where(owner == f, grams[f * double : f * double + n], top)
        low = jnp.where(owner == f, grams[f * double + n : (f + 1) * double], low)
    mine_ref[0] = (top + pltpu.roll(low, lanes - n, 1)) / total_points
    mine_ref[1] = (pltpu.roll(top, lanes - n, 1) - low) / total_points

    def copy(slot, device):
        return pltpu.make_async_remote_copy(
            src_ref=mine_ref,
            dst_ref=gram_ref.at[slot],
            send_sem=send_sems.at[device],
            recv_sem=recv_sems.at[slot],
            device_id={"space": device},
            device_id_type=pl.DeviceIdType.MESH,
        )

    pl.semaphore_wait(barrier, devices - 1)
    for s in range(1, devices):
        copy(me, lax.rem(me + s, devices)).start()
    gram_ref[me] = mine_ref[...]
    for s in range(1, devices):
        other = lax.rem(me + s, devices)
        copy(other, other).wait_recv()
    gram_re = gram_ref[0, 0]
    gram_im = gram_ref[0, 1]
    for d in range(1, devices):
        gram_re = gram_re + gram_ref[d, 0]
        gram_im = gram_im + gram_ref[d, 1]
    for j in range(n):
        mr_ref[j] = pltpu.roll(gram_re, lanes - j, 1) if j else gram_re
        mi_ref[j] = pltpu.roll(gram_im, lanes - j, 1) if j else gram_im

    def apply(vec):
        out = []
        for k in range(modes):
            vr, vi = vec[k]
            wr = wi = None
            for j in range(n):
                br, bi = vr[j : j + 1], vi[j : j + 1]
                ar, ai = mr_ref[j], mi_ref[j]
                pr, pi = ar * br - ai * bi, ar * bi + ai * br
                wr = pr if wr is None else wr + pr
                wi = pi if wi is None else wi + pi
            out.append((wr, wi))
        return out

    def total(x):
        return jnp.sum(x, axis=0, keepdims=True)

    def coefs(u, w):
        return total(u[0] * w[0] + u[1] * w[1]), total(u[0] * w[1] - u[1] * w[0])

    def less(w, u, c):
        return w[0] - (u[0] * c[0] - u[1] * c[1]), w[1] - (u[0] * c[1] + u[1] * c[0])

    def sweep(_, flat):
        vec = [(flat[2 * k], flat[2 * k + 1]) for k in range(modes)]
        images = apply(vec)
        rest = list(images)
        done = []
        for k in range(modes):
            w = rest[k]
            if done:
                cs = [coefs(u, w) for u in done]
                for u, c in zip(done, cs):
                    w = less(w, u, c)
            inverse = 1.0 / jnp.sqrt(total(w[0] * w[0] + w[1] * w[1]) + epsilon)
            u = (w[0] * inverse, w[1] * inverse)
            done.append(u)
            for later in range(k + 1, modes):
                rest[later] = less(rest[later], u, coefs(u, images[later]))
        return tuple(x for u in done for x in u)

    shape = mr_ref.shape[1:]
    flat = tuple(
        jnp.broadcast_to(start_ref[c, k], shape) for k in range(modes) for c in range(2)
    )
    flat = lax.fori_loop(0, ITERS, sweep, flat)
    vec = [(flat[2 * k], flat[2 * k + 1]) for k in range(modes)]
    images = apply(vec)
    place = lax.rem(lax.broadcasted_iota(jnp.int32, (n, lanes), 1), double)
    mix_re = mix_im = jnp.zeros((n, lanes), jnp.float32)
    for k in range(modes):
        (vr, vi), (wr, wi) = vec[k], images[k]
        energy = total(vr * wr + vi * wi)
        inverse = 1.0 / jnp.sqrt(energy + epsilon)
        energy_ref[k : k + 1] = energy
        vr, vi = vr * inverse, vi * inverse
        for part, (real, imag) in enumerate(((vr, -vi), (vi, vr))):
            slot = 2 * k + part
            if slot:
                real, imag = pltpu.roll(real, slot, 1), pltpu.roll(imag, slot, 1)
            mix_re = jnp.where(place == slot, real, mix_re)
            mix_im = jnp.where(place == slot, imag, mix_im)
    mix = jnp.concatenate([mix_re, mix_im], 0).T
    width = out_ref.shape[3]
    for f in range(freqs):
        result = jnp.dot(
            mix[f * double : f * double + 2 * modes],
            spectra_ref[f],
            precision=precise,
            preferred_element_type=jnp.float32,
        )
        for c in range(columns // width):
            out_ref[c, f] = result[:, c * width : (c + 1) * width]
    for s in range(1, devices):
        copy(me, lax.rem(me + s, devices)).wait_send()


def find_modes(spectra, col_weights, start, total_points, components):
    freqs, double, columns = spectra.shape
    n = double // 2
    lanes = freqs * double
    modes = start.shape[2]
    devices = lax.axis_size("space")
    start = jnp.pad(start, ((0, 0), (0, n - start.shape[1]), (0, 0)))
    start = start.transpose(0, 2, 1)[..., None]
    spec = pl.BlockSpec(memory_space=pltpu.VMEM)
    return pl.pallas_call(
        functools.partial(modes_kernel, modes, total_points),
        out_shape=(
            jax.ShapeDtypeStruct((components, freqs, 2 * modes, columns // components), jnp.float32),
            jax.ShapeDtypeStruct((modes, lanes), jnp.float32),
        ),
        in_specs=[spec] * 3,
        out_specs=(spec, spec),
        scratch_shapes=[
            pltpu.VMEM((devices, 2, n, lanes), jnp.float32),
            pltpu.VMEM((2, n, lanes), jnp.float32),
            pltpu.VMEM((n, n, lanes), jnp.float32),
            pltpu.VMEM((n, n, lanes), jnp.float32),
            pltpu.SemaphoreType.DMA((devices,)),
            pltpu.SemaphoreType.DMA((devices,)),
        ],
        compiler_params=pltpu.CompilerParams(
            collective_id=1, has_side_effects=True, vmem_limit_bytes=40 * 1024 * 1024
        ),
    )(spectra, col_weights, start)


def body(snapshots, weights, start):
    seg_len, components, points = snapshots.shape
    columns = components * points
    samples = snapshots.transpose(1, 0, 2)
    owners = lax.axis_size("tm")
    freqs = NF // owners
    table = segment_table(owners, seg_len)
    main, edges = exchange(table, samples)
    main = main.reshape(owners, 2, freqs, columns)
    edges = edges.reshape(owners, 2, 2, 1, columns)
    arrived = jnp.concatenate([edges[:, 0], main, edges[:, 1]], 2)
    first = lax.axis_index("tm") * freqs - 1
    signs = 1.0 - 2.0 * jnp.mod(first + owners * freqs * 2 + jnp.arange(freqs + 2), 2).astype(jnp.float32)
    pairs = arrived[:-1] + signs[:, None] * arrived[1:]
    spectra = 0.5 * pairs[..., 1:-1, :] - 0.25 * (pairs[..., :-2, :] + pairs[..., 2:, :])
    blocks = owners - 1
    padded = (blocks + 7) // 8 * 8
    spectra = jnp.pad(spectra, ((0, padded - blocks), (0, 0), (0, 0), (0, 0)))
    col_weights = jnp.tile(weights, components)[None]
    total_points = points * lax.axis_size("space")
    spectra = spectra.transpose(2, 1, 0, 3).reshape(freqs, 2 * padded, columns)
    modes, energy = find_modes(spectra, col_weights, start, total_points, components)
    modes = modes.reshape(components, freqs, start.shape[2], 2, points).transpose(1, 2, 3, 0, 4)
    return modes, energy[:, :: 2 * padded].T


def solution(mesh):
    in_specs = (P("tm", None, "space"), P("space"), P())
    out_specs = (P("tm", None, None, None, "space"), P("tm", None))
    return jax.shard_map(body, mesh=mesh, in_specs=in_specs, out_specs=out_specs, check_vma=False)
```

```python
import functools
import math

import numpy as np
import jax
import jax.numpy as jnp
from jax import lax
from jax.experimental import pallas as pl
from jax.experimental.pallas import tpu as pltpu
from jax.sharding import PartitionSpec as P

NF = 64
ITERS = 8

precise = lax.Precision.HIGHEST
epsilon = 1e-06


def segment_table(owners, seg_len):
    length = 2 * seg_len
    per = NF // owners
    t = np.arange(length)
    hann = 0.5 - 0.5 * np.cos(2.0 * np.pi / length * t)
    factor = 1.0 / np.sqrt(np.sum(hann * hann))
    freqs = np.arange(owners)[:, None] * per + np.arange(-1, per + 1)[None, :]
    turns = np.mod(freqs[:, :, None] * np.arange(seg_len), length)
    phase = 2.0 * np.pi / length * turns
    table = np.stack([np.cos(phase), -np.sin(phase)], 1) * factor
    return table.astype(np.float32)


def exchange_kernel(
    table_ref, samples_ref, main_ref, edges_ref, main_out, edge_out, forward_out,
    main_send, main_recv, edge_send, edge_recv, forward_send, forward_recv, last_send,
):
    owners, count, _ = main_ref.shape
    freqs = count // 2
    points = samples_ref.shape[2]
    quarter = edges_ref.shape[3]
    group = owners // 2
    me = lax.axis_index("tm")
    near = me // group
    far = 1 - near
    last = owners - 1

    barrier = pltpu.get_barrier_semaphore()

    @pl.loop(1, owners)
    def _(s):
        other = lax.rem(me + s, owners)
        pl.semaphore_signal(barrier, inc=1, device_id={"tm": other}, device_id_type=pl.DeviceIdType.MESH)

    def remote(source, target, sent, received, device):
        return pltpu.make_async_remote_copy(
            src_ref=source,
            dst_ref=target,
            send_sem=sent,
            recv_sem=received,
            device_id={"tm": device},
            device_id_type=pl.DeviceIdType.MESH,
        )

    def transform(side, edged):
        for c in range(samples_ref.shape[0]):
            part = jnp.dot(
                table_ref[side],
                samples_ref[c],
                precision=precise,
                preferred_element_type=jnp.float32,
            )
            low, high = c * points, (c + 1) * points
            for i in range(group):
                main_out[side * group + i, :, low:high] = part[i * count : (i + 1) * count]
            for q in range(4):
                begin, end = max(low, q * quarter), min(high, (q + 1) * quarter)
                if begin >= end:
                    continue
                for i in edged:
                    for edge in range(2):
                        for r in range(2):
                            row = group * count + i * 4 + edge * 2 + r
                            edge_out[
                                side * group + i,
                                edge,
                                r * 4 + q : r * 4 + q + 1,
                                begin - q * quarter : end - q * quarter,
                            ] = part[row : row + 1, begin - low : end - low]

    def main_copy(slot, device):
        return remote(main_out.at[device], main_ref.at[slot], main_send.at[device], main_recv.at[slot], device)

    def edge_copy(slot, device):
        return remote(edge_out.at[device], edges_ref.at[slot], edge_send.at[device], edge_recv.at[slot], device)

    def last_copy():
        return remote(
            edge_out.at[last, 1], edges_ref.at[me, 1], last_send.at[0], forward_recv.at[me, 1], last
        )

    def forward_copy(source, edge, device):
        return remote(
            forward_out.at[source, edge],
            edges_ref.at[source, edge],
            forward_send.at[source, edge],
            forward_recv.at[source, edge],
            device,
        )

    def pack(target, source, edge, freq, sign):
        for r in range(2):
            for q in range(4):
                row = main_ref[source, r * freqs + freq : r * freqs + freq + 1, q * quarter : (q + 1) * quarter]
                target[source, edge, r * 4 + q : r * 4 + q + 1, :] = row if r == 0 else sign * row

    transform(far, [group - 1])
    pl.semaphore_wait(barrier, owners - 1)

    @pl.loop(0, group)
    def _(s):
        main_copy(me, far * group + lax.rem(me + s, group)).start()

    @pl.when(near == 0)
    def _():
        last_copy().start()

    transform(near, range(group))

    @pl.loop(1, group)
    def _(s):
        other = near * group + lax.rem(me + s, group)
        main_copy(me, other).start()
        edge_copy(me, other).start()

    main_ref[me] = main_out[me]
    edges_ref[me] = edge_out[me]

    lower = me - 1
    upper = me + 1
    inner_lower = jnp.logical_and(me > 0, lower // group == near)
    inner_upper = jnp.logical_and(me < last, upper // group == near)
    outer_lower = jnp.logical_and(me > 0, lower // group != near)
    outer_upper = jnp.logical_and(me < last, upper // group != near)

    def forward(source, to_lower, to_upper):
        @pl.when(to_lower)
        def _():
            pack(forward_out, source, 1, 0, 1.0)
            forward_copy(source, 1, lower).start()

        @pl.when(to_upper)
        def _():
            pack(forward_out, source, 0, freqs - 1, 1.0)
            forward_copy(source, 0, upper).start()

    @pl.loop(0, group)
    def _(s):
        source = far * group + lax.rem(me - s + owners, group)
        main_copy(source, source).wait_recv()
        forward(source, inner_lower, inner_upper)

    forward(me, outer_lower, outer_upper)

    @pl.loop(1, group)
    def _(s):
        source = near * group + lax.rem(me - s + owners, group)
        main_copy(source, source).wait_recv()
        edge_copy(source, source).wait_recv()
        forward(source, outer_lower, outer_upper)

    @pl.loop(0, group)
    def _(s):
        source = far * group + s
        main_copy(me, source).wait_send()
        forward_copy(source, 1, lower).wait_recv()

        @pl.when(me > 0)
        def _():
            forward_copy(source, 0, upper).wait_recv()

        @pl.when(me == 0)
        def _():
            if freqs > 1:
                pack(edges_ref, source, 0, 1, -1.0)
            else:
                edges_ref[source, 0, 0:4] = edges_ref[source, 1, 0:4]
                edges_ref[source, 0, 4:8] = -edges_ref[source, 1, 4:8]

        @pl.when(inner_lower)
        def _():
            forward_copy(source, 1, lower).wait_send()

        @pl.when(inner_upper)
        def _():
            forward_copy(source, 0, upper).wait_send()

    @pl.loop(0, group)
    def _(s):
        source = near * group + s

        @pl.when(source != me)
        def _():
            main_copy(me, source).wait_send()
            edge_copy(me, source).wait_send()

        @pl.when(outer_lower)
        def _():
            forward_copy(source, 1, lower).wait_send()

        @pl.when(outer_upper)
        def _():
            forward_copy(source, 0, upper).wait_send()

    @pl.when(near == 0)
    def _():
        last_copy().wait_send()


def exchange(table, samples):
    owners, parts, freqs, seg_len = table.shape
    group = owners // 2
    columns = samples.shape[0] * samples.shape[2]
    main = table[:, :, 1:-1].reshape(2, -1, seg_len)
    edge = table[:, :, [0, freqs - 1]].swapaxes(1, 2).reshape(2, -1, seg_len)
    rows = np.concatenate([main, edge], 1)
    main_shape = (owners, parts * (freqs - 2), columns)
    edge_shape = (owners, 2, 8, columns // 4)
    spec = pl.BlockSpec(memory_space=pltpu.VMEM)
    return pl.pallas_call(
        exchange_kernel,
        out_shape=(
            jax.ShapeDtypeStruct(main_shape, jnp.float32),
            jax.ShapeDtypeStruct(edge_shape, jnp.float32),
        ),
        in_specs=[spec] * 2,
        out_specs=(spec, spec),
        scratch_shapes=[
            pltpu.VMEM(main_shape, jnp.float32),
            pltpu.VMEM(edge_shape, jnp.float32),
            pltpu.VMEM(edge_shape, jnp.float32),
            pltpu.SemaphoreType.DMA((owners,)),
            pltpu.SemaphoreType.DMA((owners,)),
            pltpu.SemaphoreType.DMA((owners,)),
            pltpu.SemaphoreType.DMA((owners,)),
            pltpu.SemaphoreType.DMA((owners, 2)),
            pltpu.SemaphoreType.DMA((owners, 2)),
            pltpu.SemaphoreType.DMA((1,)),
        ],
        compiler_params=pltpu.CompilerParams(
            collective_id=0, has_side_effects=True, vmem_limit_bytes=40 * 1024 * 1024
        ),
    )(rows, samples)


def modes_kernel(
    modes, total_points, spectra_ref, weights_ref, start_ref, out_ref, energy_ref,
    gram_ref, mine_ref, mr_ref, mi_ref, send_sems, recv_sems,
):
    freqs, double, columns = spectra_ref.shape
    n = double // 2
    lanes = freqs * double
    devices = gram_ref.shape[0]
    me = lax.axis_index("space")

    barrier = pltpu.get_barrier_semaphore()
    for s in range(1, devices):
        other = lax.rem(me + s, devices)
        pl.semaphore_signal(barrier, inc=1, device_id={"space": other}, device_id_type=pl.DeviceIdType.MESH)

    rows = spectra_ref[...].reshape(lanes, columns)
    grams = lax.dot_general(
        rows,
        rows * weights_ref[...],
        (((1,), (1,)), ((), ())),
        precision=precise,
        preferred_element_type=jnp.float32,
    )
    owner = lax.broadcasted_iota(jnp.int32, (n, lanes), 1) // double
    top = grams[:n]
    low = grams[n:double]
    for f in range(1, freqs):
        top = jnp.where(owner == f, grams[f * double : f * double + n], top)
        low = jnp.where(owner == f, grams[f * double + n : (f + 1) * double], low)
    mine_ref[0] = (top + pltpu.roll(low, lanes - n, 1)) / total_points
    mine_ref[1] = (pltpu.roll(top, lanes - n, 1) - low) / total_points

    def copy(slot, device):
        return pltpu.make_async_remote_copy(
            src_ref=mine_ref,
            dst_ref=gram_ref.at[slot],
            send_sem=send_sems.at[device],
            recv_sem=recv_sems.at[slot],
            device_id={"space": device},
            device_id_type=pl.DeviceIdType.MESH,
        )

    pl.semaphore_wait(barrier, devices - 1)
    for s in range(1, devices):
        copy(me, lax.rem(me + s, devices)).start()
    gram_ref[me] = mine_ref[...]
    for s in range(1, devices):
        other = lax.rem(me + s, devices)
        copy(other, other).wait_recv()
    gram_re = gram_ref[0, 0]
    gram_im = gram_ref[0, 1]
    for d in range(1, devices):
        gram_re = gram_re + gram_ref[d, 0]
        gram_im = gram_im + gram_ref[d, 1]
    for j in range(n):
        mr_ref[j] = pltpu.roll(gram_re, lanes - j, 1) if j else gram_re
        mi_ref[j] = pltpu.roll(gram_im, lanes - j, 1) if j else gram_im

    def apply(vec):
        out = []
        for k in range(modes):
            vr, vi = vec[k]
            wr = wi = None
            for j in range(n):
                br, bi = vr[j : j + 1], vi[j : j + 1]
                ar, ai = mr_ref[j], mi_ref[j]
                pr, pi = ar * br - ai * bi, ar * bi + ai * br
                wr = pr if wr is None else wr + pr
                wi = pi if wi is None else wi + pi
            out.append((wr, wi))
        return out

    def total(x):
        return jnp.sum(x, axis=0, keepdims=True)

    def coefs(u, w):
        return total(u[0] * w[0] + u[1] * w[1]), total(u[0] * w[1] - u[1] * w[0])

    def less(w, u, c):
        return w[0] - (u[0] * c[0] - u[1] * c[1]), w[1] - (u[0] * c[1] + u[1] * c[0])

    def sweep(_, flat):
        vec = [(flat[2 * k], flat[2 * k + 1]) for k in range(modes)]
        images = apply(vec)
        rest = list(images)
        done = []
        for k in range(modes):
            w = rest[k]
            if done:
                cs = [coefs(u, w) for u in done]
                for u, c in zip(done, cs):
                    w = less(w, u, c)
            inverse = 1.0 / jnp.sqrt(total(w[0] * w[0] + w[1] * w[1]) + epsilon)
            u = (w[0] * inverse, w[1] * inverse)
            done.append(u)
            for later in range(k + 1, modes):
                rest[later] = less(rest[later], u, coefs(u, images[later]))
        return tuple(x for u in done for x in u)

    shape = mr_ref.shape[1:]
    flat = tuple(
        jnp.broadcast_to(start_ref[c, k], shape) for k in range(modes) for c in range(2)
    )
    flat = lax.fori_loop(0, ITERS, sweep, flat)
    vec = [(flat[2 * k], flat[2 * k + 1]) for k in range(modes)]
    images = apply(vec)
    place = lax.rem(lax.broadcasted_iota(jnp.int32, (n, lanes), 1), double)
    mix_re = mix_im = jnp.zeros((n, lanes), jnp.float32)
    for k in range(modes):
        (vr, vi), (wr, wi) = vec[k], images[k]
        energy = total(vr * wr + vi * wi)
        inverse = 1.0 / jnp.sqrt(energy + epsilon)
        energy_ref[k : k + 1] = energy
        vr, vi = vr * inverse, vi * inverse
        for part, (real, imag) in enumerate(((vr, -vi), (vi, vr))):
            slot = 2 * k + part
            if slot:
                real, imag = pltpu.roll(real, slot, 1), pltpu.roll(imag, slot, 1)
            mix_re = jnp.where(place == slot, real, mix_re)
            mix_im = jnp.where(place == slot, imag, mix_im)
    mix = jnp.concatenate([mix_re, mix_im], 0).T
    width = out_ref.shape[4]
    for f in range(freqs):
        result = jnp.dot(
            mix[f * double : f * double + 2 * modes],
            spectra_ref[f],
            precision=precise,
            preferred_element_type=jnp.float32,
        )
        for c in range(columns // width):
            for k in range(modes):
                out_ref[f, k, c] = result[2 * k : 2 * k + 2, c * width : (c + 1) * width]
    for s in range(1, devices):
        copy(me, lax.rem(me + s, devices)).wait_send()


def find_modes(spectra, col_weights, start, total_points, components):
    freqs, double, columns = spectra.shape
    n = double // 2
    lanes = freqs * double
    modes = start.shape[2]
    devices = lax.axis_size("space")
    start = jnp.pad(start, ((0, 0), (0, n - start.shape[1]), (0, 0)))
    start = start.transpose(0, 2, 1)[..., None]
    spec = pl.BlockSpec(memory_space=pltpu.VMEM)
    return pl.pallas_call(
        functools.partial(modes_kernel, modes, total_points),
        out_shape=(
            jax.ShapeDtypeStruct((freqs, modes, components, 2, columns // components), jnp.float32),
            jax.ShapeDtypeStruct((modes, lanes), jnp.float32),
        ),
        in_specs=[spec] * 3,
        out_specs=(spec, spec),
        scratch_shapes=[
            pltpu.VMEM((devices, 2, n, lanes), jnp.float32),
            pltpu.VMEM((2, n, lanes), jnp.float32),
            pltpu.VMEM((n, n, lanes), jnp.float32),
            pltpu.VMEM((n, n, lanes), jnp.float32),
            pltpu.SemaphoreType.DMA((devices,)),
            pltpu.SemaphoreType.DMA((devices,)),
        ],
        compiler_params=pltpu.CompilerParams(
            collective_id=1, has_side_effects=True, vmem_limit_bytes=40 * 1024 * 1024
        ),
    )(spectra, col_weights, start)


def body(snapshots, weights, start):
    seg_len, components, points = snapshots.shape
    columns = components * points
    samples = snapshots.transpose(1, 0, 2)
    owners = lax.axis_size("tm")
    freqs = NF // owners
    table = segment_table(owners, seg_len)
    main, edges = exchange(table, samples)
    main = main.reshape(owners, 2, freqs, columns)
    edges = edges.reshape(owners, 2, 2, 1, columns)
    arrived = jnp.concatenate([edges[:, 0], main, edges[:, 1]], 2)
    first = lax.axis_index("tm") * freqs - 1
    signs = 1.0 - 2.0 * jnp.mod(first + owners * freqs * 2 + jnp.arange(freqs + 2), 2).astype(jnp.float32)
    pairs = arrived[:-1] + signs[:, None] * arrived[1:]
    spectra = 0.5 * pairs[..., 1:-1, :] - 0.25 * (pairs[..., :-2, :] + pairs[..., 2:, :])
    blocks = owners - 1
    padded = (blocks + 7) // 8 * 8
    spectra = jnp.pad(spectra, ((0, padded - blocks), (0, 0), (0, 0), (0, 0)))
    col_weights = jnp.tile(weights, components)[None]
    total_points = points * lax.axis_size("space")
    spectra = spectra.transpose(2, 1, 0, 3).reshape(freqs, 2 * padded, columns)
    modes, energy = find_modes(spectra, col_weights, start, total_points, components)
    modes = modes.swapaxes(2, 3)
    return modes, energy[:, :: 2 * padded].T


def solution(mesh):
    in_specs = (P("tm", None, "space"), P("space"), P())
    out_specs = (P("tm", None, None, None, "space"), P("tm", None))
    return jax.shard_map(body, mesh=mesh, in_specs=in_specs, out_specs=out_specs, check_vma=False)
```
